512 devices in a mesh: row: 64 (over y, z), col: 8 (over x, core).
Axes of the slice: x: 4, y: 4, z: 16, core: 2. Of those that a mesh axis runs over, the one named last changes fastest.
Arguments:
- inputs: bfloat16 [512, 8192], P(None, 'col'), may hold values from -6 to 6
- out_grad: bfloat16 [512, 8192], P(None, 'col'), may hold values from -6 to 6
- gate_weight: bfloat16 [8192, 16384], P('col', 'row'), may hold values from -0.0625 to 0.0625
- up_weight: bfloat16 [8192, 16384], P('col', 'row'), may hold values from -0.0625 to 0.0625
- down_weight: bfloat16 [16384, 8192], P('row', 'col'), may hold values from -0.046875 to 0.046875
Outputs:
- input_grad: bfloat16 [512, 8192], P('row', 'col')
- gate_wgrad: bfloat16 [8192, 16384], P('col', 'row')
- up_wgrad: bfloat16 [8192, 16384], P('col', 'row')
- down_wgrad: bfloat16 [16384, 8192], P('row', 'col')
The draws below stay inside these ranges and needn't reach their ends.
All inputs are finite; a program needn't handle non-finite values.
Results may differ from the reference program's by a relative error of at most 0.005.
Values may be sent and summed in bfloat16 or wider, within the bound.
No kernel may reach another device: no remote copies, remote signals or barrier semaphores. Data moves between devices by JAX's collectives and lax.ppermute only.
A program may use at most 64 MiB of HBM per device.

```python
import math
import jax
import jax.numpy as jnp
from jax import lax

D = 8192
FF = 16384
TOKENS = 512


def level_of(rng, shape, split, smallest, largest):
    gain = 1.0
    for dim, parts in split:
        steps = jax.random.uniform(jax.random.fold_in(jax.random.fold_in(rng, 6), dim), (parts,), jnp.float32, smallest / len(split), largest / len(split))
        gain = gain * jnp.repeat(jnp.exp(steps), shape[dim] // parts).reshape((-1,) + (1,) * (len(shape) - 1 - dim))
    return gain


def centred(own_key, shape, spread, most, cuts=(), kind=jnp.bfloat16):
    entries = jax.random.normal(own_key, shape, jnp.float32) * spread
    if len(cuts) > 0:
        entries = level_of(own_key, shape, cuts, -0.22, 0.18) * entries
    return jnp.clip(entries, min=-most, max=most).astype(kind)


def setup_inputs(seed: int = 0) -> dict:
    key_of = jax.random.split(jax.random.key(seed), 6)
    return {
        "inputs": centred(key_of[0], (TOKENS, D), 1.0, 6.0, ((1, 8),)),
        "out_grad": centred(key_of[1], (TOKENS, D), 1.0, 6.0, ((1, 8),)),
        "gate_weight": centred(key_of[2], (D, FF), D ** -0.5, 0.0625, ((0, 8), (1, 64))),
        "up_weight": centred(key_of[3], (D, FF), D ** -0.5, 0.0625, ((0, 8), (1, 64))),
        "down_weight": centred(key_of[4], (FF, D), FF ** -0.5, 0.046875, ((0, 64), (1, 8))),
    }


def reference(inputs, out_grad, gate_weight, up_weight, down_weight):
    scale = 1.0 / math.sqrt(TOKENS)
    gate = jnp.dot(inputs, gate_weight, preferred_element_type=jnp.float32)
    up = jnp.dot(inputs, up_weight, preferred_element_type=jnp.float32)
    act_grad = lax.dot_general(out_grad, down_weight, (((1,), (1,)), ((), ())), preferred_element_type=jnp.float32)
    sig = jax.nn.sigmoid(gate)
    hidden = (gate * sig * up).astype(jnp.bfloat16)
    up_grad = (act_grad * gate * sig).astype(jnp.bfloat16)
    gate_grad = (act_grad * up * sig * (1.0 + gate * (1.0 - sig))).astype(jnp.bfloat16)
    down_wgrad = (lax.dot_general(hidden, out_grad, (((0,), (0,)), ((), ())), preferred_element_type=jnp.float32) * scale).astype(jnp.bfloat16)
    gate_wgrad = (lax.dot_general(inputs, gate_grad, (((0,), (0,)), ((), ())), preferred_element_type=jnp.float32) * scale).astype(jnp.bfloat16)
    up_wgrad = (lax.dot_general(inputs, up_grad, (((0,), (0,)), ((), ())), preferred_element_type=jnp.float32) * scale).astype(jnp.bfloat16)
    back = lax.dot_general(gate_grad, gate_weight, (((1,), (1,)), ((), ())), preferred_element_type=jnp.float32)
    back = back + lax.dot_general(up_grad, up_weight, (((1,), (1,)), ((), ())), preferred_element_type=jnp.float32)
    return (back.astype(jnp.bfloat16), gate_wgrad, up_wgrad, down_wgrad)
```

```python
import math

import jax
import jax.numpy as jnp
from jax import lax
from jax.sharding import Mesh, PartitionSpec as P

TOKENS = 512
COL = ("x", "core")
ROW = ("y", "z")


def swiglu_back(gate, up, act_grad):
    sig = jax.nn.sigmoid(gate)
    hidden = (gate * sig * up).astype(jnp.bfloat16)
    up_grad = (act_grad * gate * sig).astype(jnp.bfloat16)
    gate_grad = (act_grad * up * sig * (1.0 + gate * (1.0 - sig))).astype(jnp.bfloat16)
    return (hidden, gate_grad, up_grad)


def weight_term(left, right, scale):
    return (
        lax.dot_general(left, right, (((0,), (0,)), ((), ())), preferred_element_type=jnp.float32)
        * scale
    ).astype(jnp.bfloat16)


def back_term(gate_grad, up_grad, gate_weight, up_weight):
    total = lax.dot_general(
        gate_grad, gate_weight, (((1,), (1,)), ((), ())), preferred_element_type=jnp.float32
    )
    return total + lax.dot_general(
        up_grad, up_weight, (((1,), (1,)), ((), ())), preferred_element_type=jnp.float32
    )


def sum_scatter(terms, axis, parts):
    rows = terms.shape[0] // parts
    pieces = lax.all_to_all(terms.reshape((parts, rows) + terms.shape[1:]), axis, 0, 0)
    return jnp.sum(pieces.astype(jnp.float32), axis=0)


def per_device(inputs, out_grad, gate_weight, up_weight, down_weight):
    scale = 1.0 / math.sqrt(TOKENS)
    gate_part = jnp.dot(inputs, gate_weight, preferred_element_type=jnp.float32)
    up_part = jnp.dot(inputs, up_weight, preferred_element_type=jnp.float32)
    act_part = lax.dot_general(
        out_grad, down_weight, (((1,), (1,)), ((), ())), preferred_element_type=jnp.float32
    )
    units = gate_part.shape[1]
    parts = jnp.concatenate([gate_part, up_part, act_part], axis=1).astype(jnp.bfloat16)
    sums = sum_scatter(parts, COL, 8)
    own = swiglu_back(sums[:, :units], sums[:, units : 2 * units], sums[:, 2 * units :])
    whole = lax.all_gather(jnp.concatenate(own, axis=1), COL, axis=0, tiled=True)
    hidden, gate_grad, up_grad = (
        whole[:, :units],
        whole[:, units : 2 * units],
        whole[:, 2 * units :],
    )
    terms = back_term(gate_grad, up_grad, gate_weight, up_weight).astype(jnp.bfloat16)
    near = sum_scatter(terms, "y", 4).astype(jnp.bfloat16)
    input_grad = sum_scatter(near, "z", 16)
    down_wgrad = weight_term(hidden, out_grad, scale)
    gate_wgrad = weight_term(inputs, gate_grad, scale)
    up_wgrad = weight_term(inputs, up_grad, scale)
    return (input_grad.astype(jnp.bfloat16), gate_wgrad, up_wgrad, down_wgrad)


def solution(mesh):
    grid = Mesh(mesh.devices.reshape(4, 16, 4, 2), ("y", "z", "x", "core"))
    return jax.shard_map(
        per_device,
        mesh=grid,
        in_specs=(P(None, COL), P(None, COL), P(COL, ROW), P(COL, ROW), P(ROW, COL)),
        out_specs=(P(ROW, COL), P(COL, ROW), P(COL, ROW), P(ROW, COL)),
        check_vma=False,
    )
```

```python
import math

import jax
import jax.numpy as jnp
from jax import lax
from jax.sharding import Mesh, PartitionSpec as P

TOKENS = 512
COL = ("x", "core")
ROW = ("y", "zhigh", "zlow")


def swiglu_back(gate, up, act_grad):
    sig = jax.nn.sigmoid(gate)
    hidden = (gate * sig * up).astype(jnp.bfloat16)
    up_grad = (act_grad * gate * sig).astype(jnp.bfloat16)
    gate_grad = (act_grad * up * sig * (1.0 + gate * (1.0 - sig))).astype(jnp.bfloat16)
    return (hidden, gate_grad, up_grad)


def weight_term(left, right, scale):
    return (
        lax.dot_general(left, right, (((0,), (0,)), ((), ())), preferred_element_type=jnp.float32)
        * scale
    ).astype(jnp.bfloat16)


def back_term(gate_grad, up_grad, gate_weight, up_weight):
    total = lax.dot_general(
        gate_grad, gate_weight, (((1,), (1,)), ((), ())), preferred_element_type=jnp.float32
    )
    return total + lax.dot_general(
        up_grad, up_weight, (((1,), (1,)), ((), ())), preferred_element_type=jnp.float32
    )


def sum_scatter(terms, axis, parts):
    rows = terms.shape[0] // parts
    pieces = lax.all_to_all(terms.reshape((parts, rows) + terms.shape[1:]), axis, 0, 0)
    return jnp.sum(pieces.astype(jnp.float32), axis=0)


def by_pair(rows):
    parts = rows.reshape((4, 8, 2, 8) + rows.shape[1:])
    return jnp.swapaxes(parts, 1, 2).reshape(rows.shape)


def per_device(inputs, out_grad, gate_weight, up_weight, down_weight):
    scale = 1.0 / math.sqrt(TOKENS)
    gate_part = jnp.dot(inputs, gate_weight, preferred_element_type=jnp.float32)
    up_part = jnp.dot(inputs, up_weight, preferred_element_type=jnp.float32)
    act_part = lax.dot_general(
        out_grad, down_weight, (((1,), (1,)), ((), ())), preferred_element_type=jnp.float32
    )
    units = gate_part.shape[1]
    parts = jnp.concatenate([gate_part, up_part, act_part], axis=1).astype(jnp.bfloat16)
    sums = sum_scatter(parts, COL, 8)
    own = swiglu_back(sums[:, :units], sums[:, units : 2 * units], sums[:, 2 * units :])
    whole = lax.all_gather(jnp.concatenate(own, axis=1), COL, axis=0, tiled=True)
    hidden, gate_grad, up_grad = (
        whole[:, :units],
        whole[:, units : 2 * units],
        whole[:, 2 * units :],
    )
    terms = back_term(by_pair(gate_grad), by_pair(up_grad), gate_weight, up_weight)
    near = sum_scatter(terms.astype(jnp.bfloat16), ("y", "zlow"), 8).astype(jnp.bfloat16)
    input_grad = sum_scatter(near, "zhigh", 8)
    down_wgrad = weight_term(hidden, out_grad, scale)
    gate_wgrad = weight_term(inputs, gate_grad, scale)
    up_wgrad = weight_term(inputs, up_grad, scale)
    return (input_grad.astype(jnp.bfloat16), gate_wgrad, up_wgrad, down_wgrad)


def solution(mesh):
    grid = Mesh(mesh.devices.reshape(4, 8, 2, 4, 2), ("y", "zhigh", "zlow", "x", "core"))
    return jax.shard_map(
        per_device,
        mesh=grid,
        in_specs=(P(None, COL), P(None, COL), P(COL, ROW), P(COL, ROW), P(ROW, COL)),
        out_specs=(P(ROW, COL), P(COL, ROW), P(COL, ROW), P(ROW, COL)),
        check_vma=False,
    )
```

```python
import math

import jax
import jax.numpy as jnp
from jax import lax
from jax.experimental import pallas as pl
from jax.experimental.pallas import tpu as pltpu
from jax.sharding import Mesh, PartitionSpec as P

TOKENS = 512
COL = ("x", "core")
ROW = ("y", "zhigh", "zlow")
CHUNKS = 4
NT = (((1,), (1,)), ((), ()))


def swiglu_back(gate, up, act_grad):
    sig = jax.nn.sigmoid(gate)
    hidden = (gate * sig * up).astype(jnp.bfloat16)
    up_grad = (act_grad * gate * sig).astype(jnp.bfloat16)
    gate_grad = (act_grad * up * sig * (1.0 + gate * (1.0 - sig))).astype(jnp.bfloat16)
    return (hidden, gate_grad, up_grad)


def weight_term(left, right, scale):
    return (
        lax.dot_general(left, right, (((0,), (0,)), ((), ())), preferred_element_type=jnp.float32)
        * scale
    ).astype(jnp.bfloat16)


def forward_kernel(x_hbm, o_hbm, g_hbm, u_hbm, d_hbm, out, x, o, g, u, d, sems):
    rows = x.shape[0] // CHUNKS
    units = g.shape[1]

    def copy(src, dst, sem):
        return pltpu.make_async_copy(src, dst, sems.at[sem])

    def part(i):
        return pl.ds(i * rows, rows)

    weights = [copy(g_hbm, g, 0), copy(u_hbm, u, 1), copy(d_hbm, d, 2)]
    lefts = [copy(x_hbm.at[part(i)], x.at[part(i)], 3 + i) for i in range(CHUNKS)]
    outs = [copy(o_hbm.at[part(i)], o.at[part(i)], 3 + CHUNKS + i) for i in range(CHUNKS)]
    for c in [weights[0], lefts[0], weights[1], *lefts[1:], weights[2], *outs]:
        c.start()
    for i in range(CHUNKS):
        lefts[i].wait()
        if i == 0:
            weights[0].wait()
        out[part(i), :units] = jnp.dot(
            x[part(i)], g[...], preferred_element_type=jnp.float32
        ).astype(jnp.bfloat16)
        if i == 0:
            weights[1].wait()
        out[part(i), units : 2 * units] = jnp.dot(
            x[part(i)], u[...], preferred_element_type=jnp.float32
        ).astype(jnp.bfloat16)
    weights[2].wait()
    for i in range(CHUNKS):
        outs[i].wait()
        out[part(i), 2 * units :] = lax.dot_general(
            o[part(i)], d[...], NT, preferred_element_type=jnp.float32
        ).astype(jnp.bfloat16)


def forward(inputs, out_grad, gate_weight, up_weight, down_weight):
    tokens, units = inputs.shape[0], gate_weight.shape[1]
    arrays = (inputs, out_grad, gate_weight, up_weight, down_weight)
    return pl.pallas_call(
        forward_kernel,
        out_shape=jax.ShapeDtypeStruct((tokens, 3 * units), jnp.bfloat16),
        in_specs=[pl.BlockSpec(memory_space=pl.ANY)] * 5,
        out_specs=pl.BlockSpec(memory_space=pltpu.VMEM),
        scratch_shapes=[pltpu.VMEM(a.shape, a.dtype) for a in arrays]
        + [pltpu.SemaphoreType.DMA((3 + 2 * CHUNKS,))],
        compiler_params=pltpu.CompilerParams(vmem_limit_bytes=56 << 20),
        cost_estimate=pl.CostEstimate(
            flops=6 * tokens * units * inputs.shape[1], bytes_accessed=4500000, transcendentals=0
        ),
        name="forward",
    )(*arrays)


def back_kernel(whole, g, u, out):
    units = g.shape[1]
    step = 256
    for j in range(g.shape[0] // step):
        cols = slice(j * step, (j + 1) * step)
        terms = lax.dot_general(
            whole[:, units : 2 * units], g[cols], NT, preferred_element_type=jnp.float32
        )
        terms += lax.dot_general(
            whole[:, 2 * units :], u[cols], NT, preferred_element_type=jnp.float32
        )
        terms = jnp.swapaxes(terms.reshape(4, 8, 2, 8, step), 1, 2)
        out[:, cols] = terms.reshape(-1, step).astype(jnp.bfloat16)


def back(whole, gate_weight, up_weight):
    tokens, width = whole.shape[0], gate_weight.shape[0]
    return pl.pallas_call(
        back_kernel,
        out_shape=jax.ShapeDtypeStruct((tokens, width), jnp.bfloat16),
        in_specs=[pl.BlockSpec(memory_space=pltpu.VMEM)] * 3,
        out_specs=pl.BlockSpec(memory_space=pltpu.VMEM),
        compiler_params=pltpu.CompilerParams(vmem_limit_bytes=24 << 20),
        cost_estimate=pl.CostEstimate(
            flops=4 * tokens * gate_weight.size, bytes_accessed=2500000, transcendentals=0
        ),
        name="back",
    )(whole, gate_weight, up_weight)


def sum_scatter(terms, axis, parts):
    rows = terms.shape[0] // parts
    pieces = lax.all_to_all(terms.reshape((parts, rows) + terms.shape[1:]), axis, 0, 0)
    return jnp.sum(pieces.astype(jnp.float32), axis=0)


def per_device(inputs, out_grad, gate_weight, up_weight, down_weight):
    scale = 1.0 / math.sqrt(TOKENS)
    units = gate_weight.shape[1]
    parts = forward(inputs, out_grad, gate_weight, up_weight, down_weight)
    sums = sum_scatter(parts, COL, 8)
    own = swiglu_back(sums[:, :units], sums[:, units : 2 * units], sums[:, 2 * units :])
    whole = lax.all_gather(jnp.concatenate(own, axis=1), COL, axis=0, tiled=True)
    terms = back(whole, gate_weight, up_weight)
    near = sum_scatter(terms, ("y", "zlow"), 8).astype(jnp.bfloat16)
    whole, near = lax.optimization_barrier((whole, near))
    input_grad = sum_scatter(near, "zhigh", 8)
    down_wgrad = weight_term(whole[:, :units], out_grad, scale)
    gate_wgrad = weight_term(inputs, whole[:, units : 2 * units], scale)
    up_wgrad = weight_term(inputs, whole[:, 2 * units :], scale)
    return (input_grad.astype(jnp.bfloat16), gate_wgrad, up_wgrad, down_wgrad)


def solution(mesh):
    grid = Mesh(mesh.devices.reshape(4, 8, 2, 4, 2), ("y", "zhigh", "zlow", "x", "core"))
    return jax.shard_map(
        per_device,
        mesh=grid,
        in_specs=(P(None, COL), P(None, COL), P(COL, ROW), P(COL, ROW), P(ROW, COL)),
        out_specs=(P(ROW, COL), P(COL, ROW), P(COL, ROW), P(ROW, COL)),
        check_vma=False,
    )
```

```python
import functools
import math

import jax
import jax.numpy as jnp
from jax import lax
from jax.experimental import pallas as pl
from jax.experimental.pallas import tpu as pltpu
from jax.sharding import Mesh, PartitionSpec as P

TOKENS = 512
COL = ("x", "core")
ROW = ("y", "zhigh", "zlow")
NT = (((1,), (1,)), ((), ()))


def swiglu_back(gate, up, act_grad):
    sig = jax.nn.sigmoid(gate)
    hidden = (gate * sig * up).astype(jnp.bfloat16)
    up_grad = (act_grad * gate * sig).astype(jnp.bfloat16)
    gate_grad = (act_grad * up * sig * (1.0 + gate * (1.0 - sig))).astype(jnp.bfloat16)
    return (hidden, gate_grad, up_grad)


def weight_term(left, right, scale):
    return (
        lax.dot_general(left, right, (((0,), (0,)), ((), ())), preferred_element_type=jnp.float32)
        * scale
    ).astype(jnp.bfloat16)


def forward(inputs, out_grad, gate_weight, up_weight, down_weight):
    gate_part = jnp.dot(inputs, gate_weight, preferred_element_type=jnp.float32)
    up_part = jnp.dot(inputs, up_weight, preferred_element_type=jnp.float32)
    act_part = lax.dot_general(out_grad, down_weight, NT, preferred_element_type=jnp.float32)
    return jnp.concatenate([gate_part, up_part, act_part], axis=1).astype(jnp.bfloat16)


def back_kernel(whole, g, u, out):
    units = g.shape[1]
    step = 256
    for j in range(g.shape[0] // step):
        cols = slice(j * step, (j + 1) * step)
        terms = lax.dot_general(
            whole[:, :units], g[cols], NT, preferred_element_type=jnp.float32
        )
        terms += lax.dot_general(
            whole[:, units:], u[cols], NT, preferred_element_type=jnp.float32
        )
        terms = jnp.swapaxes(terms.reshape(4, 8, 2, 8, step), 1, 2)
        out[:, cols] = terms.reshape(-1, step).astype(jnp.bfloat16)


def back(whole, gate_weight, up_weight):
    tokens, width = whole.shape[0], gate_weight.shape[0]
    return pl.pallas_call(
        back_kernel,
        out_shape=jax.ShapeDtypeStruct((tokens, width), jnp.bfloat16),
        in_specs=[pl.BlockSpec(memory_space=pltpu.VMEM)] * 3,
        out_specs=pl.BlockSpec(memory_space=pltpu.VMEM),
        compiler_params=pltpu.CompilerParams(vmem_limit_bytes=24 << 20),
        cost_estimate=pl.CostEstimate(
            flops=4 * tokens * gate_weight.size, bytes_accessed=2500000, transcendentals=0
        ),
        name="back",
    )(whole, gate_weight, up_weight)


def sum_kernel(pieces, out, *, parts):
    terms = pieces[...].astype(jnp.float32)
    out[...] = jnp.sum(terms.reshape((parts, -1) + terms.shape[1:]), axis=0).astype(jnp.bfloat16)


def sum_pieces(pieces):
    parts, rows, width = pieces.shape
    return pl.pallas_call(
        functools.partial(sum_kernel, parts=parts),
        out_shape=jax.ShapeDtypeStruct((rows, width), jnp.bfloat16),
        in_specs=[pl.BlockSpec(memory_space=pltpu.VMEM)],
        out_specs=pl.BlockSpec(memory_space=pltpu.VMEM),
        compiler_params=pltpu.CompilerParams(vmem_limit_bytes=24 << 20),
        name="sum_pieces",
    )(pieces.reshape(parts * rows, width))


def exchange(terms, axis, parts):
    return lax.all_to_all(terms.reshape((parts, -1) + terms.shape[1:]), axis, 0, 0)


def per_device(inputs, out_grad, gate_weight, up_weight, down_weight):
    scale = 1.0 / math.sqrt(TOKENS)
    units = gate_weight.shape[1]
    parts = forward(inputs, out_grad, gate_weight, up_weight, down_weight)
    sums = jnp.sum(exchange(parts, COL, 8).astype(jnp.float32), axis=0)
    own = swiglu_back(sums[:, :units], sums[:, units : 2 * units], sums[:, 2 * units :])
    hidden, gate_grad, up_grad = own
    pair = jnp.concatenate([gate_grad, up_grad], axis=1)
    over_x = lax.all_to_all(jnp.broadcast_to(pair[None], (4,) + pair.shape), "x", 0, 0)
    whole = lax.all_gather(over_x, "core", axis=1).reshape(TOKENS, 2 * units)
    terms = back(whole, gate_weight, up_weight)
    hidden, terms = lax.optimization_barrier((hidden, terms))
    hidden = lax.all_gather(hidden, COL, axis=0, tiled=True)
    near = sum_pieces(exchange(terms, ("y", "zlow"), 8))
    whole, hidden, near = lax.optimization_barrier((whole, hidden, near))
    input_grad = sum_pieces(exchange(near, "zhigh", 8))
    down_wgrad = weight_term(hidden, out_grad, scale)
    gate_wgrad = weight_term(inputs, whole[:, :units], scale)
    up_wgrad = weight_term(inputs, whole[:, units:], scale)
    return (input_grad, gate_wgrad, up_wgrad, down_wgrad)


def solution(mesh):
    grid = Mesh(mesh.devices.reshape(4, 8, 2, 4, 2), ("y", "zhigh", "zlow", "x", "core"))
    return jax.shard_map(
        per_device,
        mesh=grid,
        in_specs=(P(None, COL), P(None, COL), P(COL, ROW), P(COL, ROW), P(ROW, COL)),
        out_specs=(P(ROW, COL), P(COL, ROW), P(COL, ROW), P(ROW, COL)),
        check_vma=False,
    )
```

```python
import functools
import math

import jax
import jax.numpy as jnp
from jax import lax
from jax.experimental import pallas as pl
from jax.experimental.pallas import tpu as pltpu
from jax.sharding import Mesh, PartitionSpec as P

TOKENS = 512
COL = ("x", "core")
ROW = ("y", "zhigh", "zlow")
NT = (((1,), (1,)), ((), ()))


def swiglu_back(gate, up, act_grad):
    sig = jax.nn.sigmoid(gate)
    hidden = (gate * sig * up).astype(jnp.bfloat16)
    up_grad = (act_grad * gate * sig).astype(jnp.bfloat16)
    gate_grad = (act_grad * up * sig * (1.0 + gate * (1.0 - sig))).astype(jnp.bfloat16)
    return (hidden, gate_grad, up_grad)


def weight_term(left, right, scale):
    return (
        lax.dot_general(left, right, (((0,), (0,)), ((), ())), preferred_element_type=jnp.float32)
        * scale
    ).astype(jnp.bfloat16)


def forward(inputs, out_grad, gate_weight, up_weight, down_weight):
    gate_part = jnp.dot(inputs, gate_weight, preferred_element_type=jnp.float32)
    out_grad, gate_part = lax.optimization_barrier((out_grad, gate_part))
    act_part = lax.dot_general(out_grad, down_weight, NT, preferred_element_type=jnp.float32)
    inputs, act_part = lax.optimization_barrier((inputs, act_part))
    up_part = jnp.dot(inputs, up_weight, preferred_element_type=jnp.float32)
    return jnp.concatenate([gate_part, up_part, act_part], axis=1).astype(jnp.bfloat16)


def back_kernel(whole, g, u, out, terms_vmem, sems):
    units = g.shape[1]
    rows, step = whole.shape[0] // 2, 256
    copies = []
    for i in range(2):
        part = pl.ds(i * rows, rows)
        for j in range(g.shape[0] // step):
            cols = pl.ds(j * step, step)
            terms = lax.dot_general(
                whole[part, :units], g[cols], NT, preferred_element_type=jnp.float32
            )
            terms += lax.dot_general(
                whole[part, units:], u[cols], NT, preferred_element_type=jnp.float32
            )
            terms = jnp.swapaxes(terms.reshape(2, 8, 2, 8, step), 1, 2)
            terms_vmem[part, cols] = terms.reshape(-1, step).astype(jnp.bfloat16)
        copies.append(pltpu.make_async_copy(terms_vmem.at[part], out.at[part], sems.at[i]))
        copies[-1].start()
    for copy in copies:
        copy.wait()


def back(whole, gate_weight, up_weight):
    tokens, width = whole.shape[0], gate_weight.shape[0]
    return pl.pallas_call(
        back_kernel,
        out_shape=jax.ShapeDtypeStruct((tokens, width), jnp.bfloat16),
        in_specs=[pl.BlockSpec(memory_space=pltpu.VMEM)] * 3,
        out_specs=pl.BlockSpec(memory_space=pl.ANY),
        scratch_shapes=[
            pltpu.VMEM((tokens, width), jnp.bfloat16),
            pltpu.SemaphoreType.DMA((width // 256,)),
        ],
        compiler_params=pltpu.CompilerParams(vmem_limit_bytes=24 << 20),
        name="back",
    )(whole, gate_weight, up_weight)


def sum_kernel(pieces, out, *, parts):
    terms = pieces[...].astype(jnp.float32)
    out[...] = jnp.sum(terms.reshape((parts, -1) + terms.shape[1:]), axis=0).astype(jnp.bfloat16)


def sum_pieces(pieces):
    parts, rows, width = pieces.shape
    return pl.pallas_call(
        functools.partial(sum_kernel, parts=parts),
        out_shape=jax.ShapeDtypeStruct((rows, width), jnp.bfloat16),
        in_specs=[pl.BlockSpec(memory_space=pltpu.VMEM)],
        out_specs=pl.BlockSpec(memory_space=pltpu.VMEM),
        compiler_params=pltpu.CompilerParams(vmem_limit_bytes=24 << 20),
        name="sum_pieces",
    )(pieces.reshape(parts * rows, width))


def exchange(terms, axis, parts):
    return lax.all_to_all(terms.reshape((parts, -1) + terms.shape[1:]), axis, 0, 0)


def per_device(inputs, out_grad, gate_weight, up_weight, down_weight):
    scale = 1.0 / math.sqrt(TOKENS)
    units = gate_weight.shape[1]
    parts = forward(inputs, out_grad, gate_weight, up_weight, down_weight)
    sums = jnp.sum(exchange(parts, COL, 8).astype(jnp.float32), axis=0)
    own = swiglu_back(sums[:, :units], sums[:, units : 2 * units], sums[:, 2 * units :])
    hidden, gate_grad, up_grad = own
    pair = jnp.concatenate([gate_grad, up_grad], axis=1)
    over_x = lax.all_to_all(jnp.broadcast_to(pair[None], (4,) + pair.shape), "x", 0, 0)
    whole = lax.all_gather(over_x, "core", axis=1).reshape(TOKENS, 2 * units)
    terms = back(whole, gate_weight, up_weight)
    hidden, terms = lax.optimization_barrier((hidden, terms))
    hidden = lax.all_gather(hidden, COL, axis=0, tiled=True)
    near = sum_pieces(exchange(terms, ("y", "zlow"), 8))
    whole, hidden, near = lax.optimization_barrier((whole, hidden, near))
    input_grad = sum_pieces(exchange(near, "zhigh", 8))
    down_wgrad = weight_term(hidden, out_grad, scale)
    gate_wgrad = weight_term(inputs, whole[:, :units], scale)
    up_wgrad = weight_term(inputs, whole[:, units:], scale)
    return (input_grad, gate_wgrad, up_wgrad, down_wgrad)


def solution(mesh):
    grid = Mesh(mesh.devices.reshape(4, 8, 2, 4, 2), ("y", "zhigh", "zlow", "x", "core"))
    return jax.shard_map(
        per_device,
        mesh=grid,
        in_specs=(P(None, COL), P(None, COL), P(COL, ROW), P(COL, ROW), P(ROW, COL)),
        out_specs=(P(ROW, COL), P(COL, ROW), P(COL, ROW), P(ROW, COL)),
        check_vma=False,
    )
```

```python
import functools
import math

import jax
import jax.numpy as jnp
from jax import lax
from jax.experimental import pallas as pl
from jax.experimental.pallas import tpu as pltpu
from jax.sharding import Mesh, PartitionSpec as P

TOKENS = 512
COL = ("x", "core")
ROW = ("y", "zhigh", "zlow")
NT = (((1,), (1,)), ((), ()))


def swiglu_back(gate, up, act_grad):
    sig = jax.nn.sigmoid(gate)
    hidden = (gate * sig * up).astype(jnp.bfloat16)
    up_grad = (act_grad * gate * sig).astype(jnp.bfloat16)
    gate_grad = (act_grad * up * sig * (1.0 + gate * (1.0 - sig))).astype(jnp.bfloat16)
    return (hidden, gate_grad, up_grad)


def weight_term(left, right, scale):
    return (
        lax.dot_general(left, right, (((0,), (0,)), ((), ())), preferred_element_type=jnp.float32)
        * scale
    ).astype(jnp.bfloat16)


def forward(inputs, out_grad, gate_weight, up_weight, down_weight):
    gate_part = jnp.dot(inputs, gate_weight, preferred_element_type=jnp.float32)
    out_grad, gate_part = lax.optimization_barrier((out_grad, gate_part))
    act_part = lax.dot_general(out_grad, down_weight, NT, preferred_element_type=jnp.float32)
    inputs, act_part = lax.optimization_barrier((inputs, act_part))
    up_part = jnp.dot(inputs, up_weight, preferred_element_type=jnp.float32)
    return jnp.concatenate([gate_part, up_part, act_part], axis=1).astype(jnp.bfloat16)


def back_kernel(whole, g, u, out):
    units = g.shape[1]
    step = 256
    for j in range(g.shape[0] // step):
        cols = slice(j * step, (j + 1) * step)
        terms = lax.dot_general(
            whole[:, units : 2 * units], g[cols], NT, preferred_element_type=jnp.float32
        )
        terms += lax.dot_general(
            whole[:, 2 * units :], u[cols], NT, preferred_element_type=jnp.float32
        )
        terms = jnp.swapaxes(terms.reshape(4, 8, 2, 8, step), 1, 2)
        out[:, cols] = terms.reshape(-1, step).astype(jnp.bfloat16)


def back(whole, gate_weight, up_weight):
    tokens, width = whole.shape[0], gate_weight.shape[0]
    return pl.pallas_call(
        back_kernel,
        out_shape=jax.ShapeDtypeStruct((tokens, width), jnp.bfloat16),
        in_specs=[pl.BlockSpec(memory_space=pltpu.VMEM)] * 3,
        out_specs=pl.BlockSpec(memory_space=pltpu.VMEM),
        compiler_params=pltpu.CompilerParams(vmem_limit_bytes=24 << 20),
        cost_estimate=pl.CostEstimate(
            flops=4 * tokens * gate_weight.size, bytes_accessed=2500000, transcendentals=0
        ),
        name="back",
    )(whole, gate_weight, up_weight)


def sum_kernel(pieces, out, *, parts):
    terms = pieces[...].astype(jnp.float32)
    out[...] = jnp.sum(terms.reshape((parts, -1) + terms.shape[1:]), axis=0).astype(jnp.bfloat16)


def sum_pieces(pieces):
    parts, rows, width = pieces.shape
    return pl.pallas_call(
        functools.partial(sum_kernel, parts=parts),
        out_shape=jax.ShapeDtypeStruct((rows, width), jnp.bfloat16),
        in_specs=[pl.BlockSpec(memory_space=pltpu.VMEM)],
        out_specs=pl.BlockSpec(memory_space=pltpu.VMEM),
        compiler_params=pltpu.CompilerParams(vmem_limit_bytes=24 << 20),
        name="sum_pieces",
    )(pieces.reshape(parts * rows, width))


def exchange(terms, axis, parts):
    return lax.all_to_all(terms.reshape((parts, -1) + terms.shape[1:]), axis, 0, 0)


def per_device(inputs, out_grad, gate_weight, up_weight, down_weight):
    scale = 1.0 / math.sqrt(TOKENS)
    units = gate_weight.shape[1]
    parts = forward(inputs, out_grad, gate_weight, up_weight, down_weight)
    sums = jnp.sum(exchange(parts, COL, 8).astype(jnp.float32), axis=0)
    own = swiglu_back(sums[:, :units], sums[:, units : 2 * units], sums[:, 2 * units :])
    own = jnp.concatenate(own, axis=1)
    over_x = lax.all_to_all(jnp.broadcast_to(own[None], (4,) + own.shape), "x", 0, 0)
    whole = lax.all_gather(over_x, "core", axis=1).reshape(TOKENS, 3 * units)
    terms = back(whole, gate_weight, up_weight)
    near = sum_pieces(exchange(terms, ("y", "zlow"), 8))
    whole, near = lax.optimization_barrier((whole, near))
    input_grad = sum_pieces(exchange(near, "zhigh", 8))
    down_wgrad = weight_term(whole[:, :units], out_grad, scale)
    gate_wgrad = weight_term(inputs, whole[:, units : 2 * units], scale)
    up_wgrad = weight_term(inputs, whole[:, 2 * units :], scale)
    return (input_grad, gate_wgrad, up_wgrad, down_wgrad)


def solution(mesh):
    grid = Mesh(mesh.devices.reshape(4, 8, 2, 4, 2), ("y", "zhigh", "zlow", "x", "core"))
    return jax.shard_map(
        per_device,
        mesh=grid,
        in_specs=(P(None, COL), P(None, COL), P(COL, ROW), P(COL, ROW), P(ROW, COL)),
        out_specs=(P(ROW, COL), P(COL, ROW), P(COL, ROW), P(ROW, COL)),
        check_vma=False,
    )
```

```python
import functools
import math

import jax
import jax.numpy as jnp
from jax import lax
from jax.experimental import pallas as pl
from jax.experimental.pallas import tpu as pltpu
from jax.sharding import Mesh, PartitionSpec as P

TOKENS = 512
COL = ("x", "core")
ROW = ("y", "zhigh", "zlow")
NT = (((1,), (1,)), ((), ()))


def swiglu_back(gate, up, act_grad):
    sig = jax.nn.sigmoid(gate)
    hidden = (gate * sig * up).astype(jnp.bfloat16)
    up_grad = (act_grad * gate * sig).astype(jnp.bfloat16)
    gate_grad = (act_grad * up * sig * (1.0 + gate * (1.0 - sig))).astype(jnp.bfloat16)
    return (hidden, gate_grad, up_grad)


def weight_term(left, right, scale):
    return (
        lax.dot_general(left, right, (((0,), (0,)), ((), ())), preferred_element_type=jnp.float32)
        * scale
    ).astype(jnp.bfloat16)


def forward(inputs, out_grad, gate_weight, up_weight, down_weight):
    gate_part = jnp.dot(inputs, gate_weight, preferred_element_type=jnp.float32)
    out_grad, gate_part = lax.optimization_barrier((out_grad, gate_part))
    act_part = lax.dot_general(out_grad, down_weight, NT, preferred_element_type=jnp.float32)
    inputs, act_part = lax.optimization_barrier((inputs, act_part))
    up_part = jnp.dot(inputs, up_weight, preferred_element_type=jnp.float32)
    return jnp.concatenate([gate_part, up_part, act_part], axis=1).astype(jnp.bfloat16)


def back_kernel(whole, g, u, out, terms_vmem, sems):
    units = g.shape[1]
    rows, step = whole.shape[0] // 2, 256
    copies = []
    for i in range(2):
        part = pl.ds(i * rows, rows)
        for j in range(g.shape[0] // step):
            cols = pl.ds(j * step, step)
            terms = lax.dot_general(
                whole[part, :units], g[cols], NT, preferred_element_type=jnp.float32
            )
            terms += lax.dot_general(
                whole[part, units:], u[cols], NT, preferred_element_type=jnp.float32
            )
            terms = jnp.swapaxes(terms.reshape(2, 8, 2, 8, step), 1, 2)
            terms_vmem[part, cols] = terms.reshape(-1, step).astype(jnp.bfloat16)
        copies.append(pltpu.make_async_copy(terms_vmem.at[part], out.at[part], sems.at[i]))
        copies[-1].start()
    for copy in copies:
        copy.wait()


def back(whole, gate_weight, up_weight):
    tokens, width = whole.shape[0], gate_weight.shape[0]
    return pl.pallas_call(
        back_kernel,
        out_shape=jax.ShapeDtypeStruct((tokens, width), jnp.bfloat16),
        in_specs=[pl.BlockSpec(memory_space=pltpu.VMEM)] * 3,
        out_specs=pl.BlockSpec(memory_space=pl.ANY),
        scratch_shapes=[
            pltpu.VMEM((tokens, width), jnp.bfloat16),
            pltpu.SemaphoreType.DMA((width // 256,)),
        ],
        compiler_params=pltpu.CompilerParams(vmem_limit_bytes=24 << 20),
        name="back",
    )(whole, gate_weight, up_weight)


def sum_kernel(pieces, out, *, parts):
    rows = pieces.shape[0] // parts
    step = 16
    if rows % step == 0:
        for r in range(0, rows, step):
            total = pieces[r : r + step].astype(jnp.float32)
            for p in range(1, parts):
                total += pieces[p * rows + r : p * rows + r + step].astype(jnp.float32)
            out[r : r + step] = total.astype(jnp.bfloat16)
    else:
        total = pieces[:step].astype(jnp.float32)
        for r in range(step, pieces.shape[0], step):
            total += pieces[r : r + step].astype(jnp.float32)
        total = jnp.sum(total.reshape((step // rows, rows) + total.shape[1:]), axis=0)
        out[...] = total.astype(jnp.bfloat16)


def sum_pieces(pieces):
    parts, rows, width = pieces.shape
    return pl.pallas_call(
        functools.partial(sum_kernel, parts=parts),
        out_shape=jax.ShapeDtypeStruct((rows, width), jnp.bfloat16),
        in_specs=[pl.BlockSpec(memory_space=pltpu.VMEM)],
        out_specs=pl.BlockSpec(memory_space=pltpu.VMEM),
        compiler_params=pltpu.CompilerParams(vmem_limit_bytes=24 << 20),
        name="sum_pieces",
    )(pieces.reshape(parts * rows, width))


def exchange(terms, axis, parts):
    return lax.all_to_all(terms.reshape((parts, -1) + terms.shape[1:]), axis, 0, 0)


def per_device(inputs, out_grad, gate_weight, up_weight, down_weight):
    scale = 1.0 / math.sqrt(TOKENS)
    units = gate_weight.shape[1]
    parts = forward(inputs, out_grad, gate_weight, up_weight, down_weight)
    sums = jnp.sum(exchange(parts, COL, 8).astype(jnp.float32), axis=0)
    own = swiglu_back(sums[:, :units], sums[:, units : 2 * units], sums[:, 2 * units :])
    hidden, gate_grad, up_grad = own
    pair = jnp.concatenate([gate_grad, up_grad], axis=1)
    over_x = lax.all_to_all(jnp.broadcast_to(pair[None], (4,) + pair.shape), "x", 0, 0)
    whole = lax.all_gather(over_x, "core", axis=1).reshape(TOKENS, 2 * units)
    terms = back(whole, gate_weight, up_weight)
    hidden, terms = lax.optimization_barrier((hidden, terms))
    hidden = lax.all_gather(hidden, COL, axis=0, tiled=True)
    near = sum_pieces(exchange(terms, ("y", "zlow"), 8))
    whole, hidden, near = lax.optimization_barrier((whole, hidden, near))
    input_grad = sum_pieces(exchange(near, "zhigh", 8))
    down_wgrad = weight_term(hidden, out_grad, scale)
    gate_wgrad = weight_term(inputs, whole[:, :units], scale)
    up_wgrad = weight_term(inputs, whole[:, units:], scale)
    return (input_grad, gate_wgrad, up_wgrad, down_wgrad)


def solution(mesh):
    grid = Mesh(mesh.devices.reshape(4, 8, 2, 4, 2), ("y", "zhigh", "zlow", "x", "core"))
    return jax.shard_map(
        per_device,
        mesh=grid,
        in_specs=(P(None, COL), P(None, COL), P(COL, ROW), P(COL, ROW), P(ROW, COL)),
        out_specs=(P(ROW, COL), P(COL, ROW), P(COL, ROW), P(ROW, COL)),
        check_vma=False,
    )
```
